32 devices in a mesh: lon: 8 (over z, y), lat: 4 (over x, core).
Axes of the slice: x: 2, y: 2, z: 4, core: 2. Of those that a mesh axis runs over, the one named last changes fastest.
Arguments:
- wind_u: float32 [720, 1440, 16], P('lat', 'lon'), may hold values from -6 to 6
- wind_v: float32 [720, 1440, 16], P('lat', 'lon'), may hold values from -6 to 6
- vorticity: float32 [720, 1440, 16], P('lat', 'lon'), may hold values from -6 to 6
- sample_level: int32 [16], replicated, may hold values from 0 to 1, as said below
- slot_wavenumber: int32 [720], P('lon'), may hold values from 0 to 719, as said below
- legendre_p: bfloat16 [720, 518400], P('lat', 'lon'), may hold values from -5 to 5
- legendre_h: bfloat16 [720, 518400], P('lat', 'lon'), may hold values from -5 to 5
Outputs:
- spectra: float32 [2, 518400], P(None, ('lon', 'lat'))
The draws below stay inside these ranges and needn't reach their ends.
Inputs may be any that keep to these rules, and one draw needn't show every extreme that they name: `sample_level`: each level is named by exactly 8 samples. `slot_wavenumber`: each wavenumber from 0 to 719 stands in exactly one slot; the remaining slots hold -1.
All inputs are finite; a program needn't handle non-finite values.
Results may differ from the reference program's by a relative error of at most 0.0014.
Values sent between devices are 32-bit elements; how exact they have to be, the bound alone decides.
No kernel may reach another device: no remote copies, remote signals or barrier semaphores. Data moves between devices by JAX's collectives and lax.ppermute only.
A program may use at most 192 MiB of HBM per device.

```python
import math
import jax
import jax.numpy as jnp
from jax import lax

NLON = 1440
NLAT = 720
MAXM = 720
LEV = 2
DAYS = 8
S = 16
SLOTS = 720


def draw_sample_level(key, part):
    order = jax.random.permutation(key, S)
    return (order % LEV).astype(jnp.int32)


def draw_slot_wavenumber(key, part):
    order = jax.random.permutation(key, SLOTS)
    return jnp.where(order < MAXM, order, -1).astype(jnp.int32)


def level_of(rng, dims, pieces, smallest, top_value):
    factor_of = 1.0
    for position, shards_of in pieces:
        draws = jax.random.uniform(jax.random.fold_in(jax.random.fold_in(rng, 6), position), (shards_of,), jnp.float32, smallest / len(pieces), top_value / len(pieces))
        factor_of = factor_of * jnp.repeat(jnp.exp(draws), dims[position] // shards_of).reshape((-1,) + (1,) * (len(dims) - 1 - position))
    return factor_of


def gaussian(stream_key, shape, deviation, reach, pieces=(), held_as=jnp.bfloat16):
    gain = level_of(stream_key, shape, pieces, -0.22, 0.18) if pieces else 1.0
    drawn = jax.random.normal(stream_key, shape, jnp.float32) * deviation * gain
    return jnp.minimum(jnp.maximum(drawn, -reach), reach).astype(held_as)


def setup_inputs(seed: int = 0) -> dict:
    streams_of = jax.random.split(jax.random.key(seed), 8)
    wind_u = gaussian(streams_of[0], (NLAT, NLON, S), 1.0, 6.0, ((0, 4), (1, 8)), jnp.float32)
    wind_v = gaussian(streams_of[1], (NLAT, NLON, S), 1.0, 6.0, ((0, 4), (1, 8)), jnp.float32)
    vorticity = gaussian(streams_of[2], (NLAT, NLON, S), 1.0, 6.0, ((0, 4), (1, 8)), jnp.float32)
    sample_level = draw_sample_level(jax.random.fold_in(streams_of[7], 71), 0)
    slot_wavenumber = draw_slot_wavenumber(jax.random.fold_in(streams_of[7], 71), 0)
    legendre_p = gaussian(streams_of[5], (NLAT, SLOTS * MAXM), 1.0, 5.0, ((0, 4), (1, 8)))
    legendre_h = gaussian(streams_of[6], (NLAT, SLOTS * MAXM), 1.0, 5.0, ((0, 4), (1, 8)))
    return dict(wind_u=wind_u, wind_v=wind_v, vorticity=vorticity, sample_level=sample_level, slot_wavenumber=slot_wavenumber, legendre_p=legendre_p, legendre_h=legendre_h)


def remove_means(field, onehot):
    means = jnp.einsum("jis,sl->jil", field, onehot, precision=lax.Precision.HIGHEST) / DAYS
    return field - jnp.einsum("jil,sl->jis", means, onehot, precision=lax.Precision.HIGHEST)


def reference(wind_u, wind_v, vorticity, sample_level, slot_wavenumber, legendre_p, legendre_h):
    onehot = (sample_level[:, None] == jnp.arange(LEV, dtype=jnp.int32)[None, :]).astype(jnp.float32)
    eddy_u = remove_means(wind_u, onehot)
    eddy_v = remove_means(wind_v, onehot)
    eddy_z = remove_means(vorticity, onehot)
    latitude = (jnp.arange(NLAT, dtype=jnp.float32) + 0.5) * (math.pi / NLAT) - 0.5 * math.pi
    cosine = jnp.cos(latitude)[:, None, None]
    fluxes = jnp.concatenate([eddy_u * eddy_z * cosine, eddy_v * eddy_z * cosine], axis=2)
    spectrum = jnp.fft.rfft(fluxes, axis=1) / NLON
    present = slot_wavenumber >= 0
    clipped = jnp.maximum(slot_wavenumber, 0).astype(jnp.int32)
    weight = present.astype(jnp.float32)[None, :, None]
    cos_part = jnp.real(spectrum)[:, clipped, :] * weight
    sin_part = -jnp.imag(spectrum)[:, clipped, :] * weight
    scale = (clipped.astype(jnp.float32) / MAXM)[None, :, None]
    right_p = jnp.concatenate([scale * sin_part[:, :, :S], scale * cos_part[:, :, :S]], axis=2).astype(jnp.bfloat16)
    right_h = jnp.concatenate([-cos_part[:, :, S:], sin_part[:, :, S:]], axis=2).astype(jnp.bfloat16)
    degree = jnp.arange(MAXM, dtype=jnp.int32)

    def per_slot(index):
        table_p = lax.dynamic_slice_in_dim(legendre_p, index * MAXM, MAXM, 1).astype(jnp.float32)
        table_h = lax.dynamic_slice_in_dim(legendre_h, index * MAXM, MAXM, 1).astype(jnp.float32)
        rhs_p = lax.dynamic_index_in_dim(right_p, index, 1, keepdims=False).astype(jnp.float32)
        rhs_h = lax.dynamic_index_in_dim(right_h, index, 1, keepdims=False).astype(jnp.float32)
        coeffs = jnp.dot(table_p.T, rhs_p, precision=lax.Precision.HIGHEST)
        coeffs = coeffs + jnp.dot(table_h.T, rhs_h, precision=lax.Precision.HIGHEST)
        keep = ((degree >= clipped[index]) & present[index]).astype(jnp.float32)
        coeffs = coeffs * keep[:, None]
        power = coeffs[:, :S] ** 2 + coeffs[:, S:] ** 2
        return jnp.dot(power, onehot, precision=lax.Precision.HIGHEST) / DAYS

    spectra = lax.map(per_slot, jnp.arange(SLOTS, dtype=jnp.int32))
    return spectra.reshape(SLOTS * MAXM, LEV).T
```

```python
import functools
import math

import jax
import jax.numpy as jnp
from jax import lax
from jax.experimental import pallas as pl
from jax.experimental.pallas import tpu as pltpu
from jax.sharding import PartitionSpec as P

NLON = 1440
NLAT = 720
MAXM = 720
LEV = 2
DAYS = 8
S = 16
LANES = 128
HALF = 64
VMEM_LIMIT = 56 * 1024 * 1024


def up(value, step):
    return -(-value // step) * step


class Plan:
    def __init__(self, rows, lons, owned, lon_count, lat_count):
        self.rows, self.lons, self.owned = rows, lons, owned
        self.n, self.lat_count = lon_count, lat_count
        self.cols = 2 * S // lon_count
        self.row_pad = up(rows, 8)
        self.stride = up(rows, HALF)
        self.full, self.rem = divmod(lons, LANES)
        assert 0 < self.rem < HALF
        pairs = 2 if self.cols % 2 == 0 else 1
        self.per_chunk = pairs
        self.chunks = self.cols // pairs
        self.blocks = pairs * self.full + 1
        self.depth = lon_count * (self.full * LANES + HALF)
        self.circles = self.cols * self.stride
        self.chunk_circles = pairs * self.stride
        self.share = owned * MAXM // lat_count
        self.first = [self.share * t // MAXM for t in range(lat_count)]
        last = [-(-self.share * (t + 1) // MAXM) for t in range(lat_count)]
        self.cover = max(b - a for a, b in zip(self.first, last))
        parts = 3
        sizes = [self.cover // parts + (1 if i < self.cover % parts else 0) for i in range(parts)]
        self.sizes = [s for s in sizes if s]
        self.starts = [sum(self.sizes[:i]) for i in range(len(self.sizes))]
        self.position_count = [lat_count * s for s in self.sizes]
        self.position_start = [lat_count * s for s in self.starts]
        slots = []
        for start, size in zip(self.starts, self.sizes):
            for t in range(lat_count):
                slots += [self.first[t] + start + i for i in range(size)]
        self.slots = slots
        assert len(slots) <= self.row_pad


def lane_iota(shape):
    return lax.broadcasted_iota(jnp.int32, shape, len(shape) - 1)


def flux_kernel(plan, tile, lev_ref, cos_ref, slot_ref, u_ref, v_ref, z_ref, *refs):
    outs, scratch = refs[:-1], refs[-1]
    me = lax.axis_index("lon")
    level = lev_ref[...]

    def eddy(x):
        out = x
        for a in range(LEV):
            mask = (level == a).astype(jnp.float32)[None]
            mean = jnp.sum(x * mask, axis=1, keepdims=True) * (1.0 / DAYS)
            out = out - mean * mask
        return out

    eddy_z = eddy(z_ref[...])
    for f, ref in enumerate((u_ref, v_ref)):
        flux = eddy(ref[...]) * eddy_z
        for b in range(plan.full):
            part = flux[:, :, b * LANES : (b + 1) * LANES]
            scratch[f, b] = part.reshape(tile * S, LANES)
        part = flux[:, :, plan.full * LANES :]
        scratch[f, plan.full, :, 0 : plan.rem] = part.reshape(tile * S, plan.rem)
    cosine = cos_ref[...]
    lane = lane_iota((tile, LANES))
    per_field = plan.n // 2
    for k in range(plan.n):
        dest = lax.bitwise_xor(me, k)
        field = dest // per_field
        sample = lax.rem(dest, per_field) * plan.cols
        for chunk in range(plan.chunks):
            out = outs[chunk * plan.n + k]
            packed = jnp.zeros((tile, LANES), jnp.float32)
            for c in range(plan.per_chunk):
                rows = pl.ds(sample + chunk * plan.per_chunk + c, tile, stride=S)
                for b in range(plan.full):
                    out[c * plan.full + b] = scratch[field, b, rows, :] * cosine
                tail = jnp.where(lane < plan.rem, scratch[field, plan.full, rows, :] * cosine, 0.0)
                if c:
                    tail = pltpu.roll(tail, HALF * c, 1)
                packed = packed + tail
            if chunk == 0:
                packed = jnp.where(lane == HALF - 1, slot_ref[...], packed)
            out[plan.per_chunk * plan.full] = packed


def flux_call(plan, level, cosine, slots, u, v, z):
    tile = min(48, plan.row_pad)
    field = pl.BlockSpec((tile, S, plan.lons), lambda i: (i, 0, 0))
    column = pl.BlockSpec((tile, 1), lambda i: (i, 0))
    return pl.pallas_call(
        functools.partial(flux_kernel, plan, tile),
        grid=(pl.cdiv(plan.row_pad, tile),),
        in_specs=[pl.BlockSpec((S, 1), lambda i: (0, 0)), column, column, field, field, field],
        out_specs=[pl.BlockSpec((plan.blocks, tile, LANES), lambda i: (0, i, 0))]
        * (plan.chunks * plan.n),
        out_shape=[jax.ShapeDtypeStruct((plan.blocks, plan.row_pad, LANES), jnp.float32)]
        * (plan.chunks * plan.n),
        scratch_shapes=[pltpu.VMEM((2, plan.full + 1, tile * S, LANES), jnp.float32)],
        compiler_params=pltpu.CompilerParams(vmem_limit_bytes=VMEM_LIMIT),
        name="eddy_flux",
    )(level, cosine, slots, u, v, z)


def sincos(x):
    r = x - NLON * jnp.floor(x * (1.0 / NLON) + 0.5)
    q = jnp.floor(r * (4.0 / NLON) + 0.5)
    t = (r - q * (NLON // 4)) * (2.0 * math.pi / NLON)
    t2 = t * t
    s = t * (1.0 + t2 * (-1.0 / 6 + t2 * (1.0 / 120 + t2 * (-1.0 / 5040 + t2 * (1.0 / 362880)))))
    c = 1.0 + t2 * (
        -0.5 + t2 * (1.0 / 24 + t2 * (-1.0 / 720 + t2 * (1.0 / 40320 + t2 * (-1.0 / 3628800))))
    )
    size = jnp.abs(q)
    odd, flip = size == 1.0, size == 2.0
    cosine = jnp.where(odd, -q * s, jnp.where(flip, -c, c))
    sine = jnp.where(odd, q * c, jnp.where(flip, -s, s))
    return cosine, sine


def table_kernel(plan, *refs):
    pieces = refs[: plan.n]
    parts = len(plan.sizes)
    highs, lows = refs[plan.n : plan.n + parts], refs[plan.n + parts : plan.n + 2 * parts]
    held = refs[-1]
    me = lax.axis_index("lon")
    for k in range(plan.n):
        held[k] = pieces[k][0]

    @pl.loop(0, plan.n)
    def _(k):
        for j, count in enumerate(plan.position_count):
            start = plan.position_start[j]
            wave = held[k, start : start + count, HALF - 1 : HALF]
            weight = jnp.where(wave >= 0.0, 1.0 / NLON, 0.0)
            wave = jnp.maximum(wave, 0.0)
            lane = lane_iota((count, LANES))
            source = lax.bitwise_xor(lane, me).astype(jnp.float32) * plan.lons
            turn_cos, turn_sin = sincos(wave * source)
            base = []
            for b in range(plan.full):
                c, s = sincos(wave * (lane + b * LANES).astype(jnp.float32))
                base.append((c * weight, s * weight))
            tail_lane = lane_iota((count, HALF))
            c, s = sincos(wave * (tail_lane + plan.full * LANES).astype(jnp.float32))
            tail_weight = jnp.where(tail_lane < plan.rem, weight, 0.0)
            c, s = c * tail_weight, s * tail_weight

            def put(where, cosine, sine):
                for row, value in ((0, cosine), (count, sine)):
                    high = value.astype(jnp.bfloat16)
                    highs[j][k, row : row + count, where] = high
                    lows[j][k, row : row + count, where] = (
                        value - high.astype(jnp.float32)
                    ).astype(jnp.bfloat16)

            for src in range(plan.n):
                tc, ts = turn_cos[:, src : src + 1], turn_sin[:, src : src + 1]
                for b in range(plan.full):
                    at = (src * plan.full + b) * LANES
                    bc, bs = base[b]
                    put(slice(at, at + LANES), tc * bc - ts * bs, ts * bc + tc * bs)
            for src in range(0, plan.n, 2):
                at = plan.n * plan.full * LANES + src * HALF
                both = []
                for x in (src, src + 1):
                    tc, ts = turn_cos[:, x : x + 1], turn_sin[:, x : x + 1]
                    both.append((tc * c - ts * s, ts * c + tc * s))
                put(
                    slice(at, at + LANES),
                    jnp.concatenate([both[0][0], both[1][0]], axis=1),
                    jnp.concatenate([both[0][1], both[1][1]], axis=1),
                )


def table_call(plan, pieces):
    tail = pl.BlockSpec((1, plan.row_pad, LANES), lambda i: (plan.blocks - 1, 0, 0))
    shapes = [
        jax.ShapeDtypeStruct((plan.n, 2 * count, plan.depth), jnp.bfloat16)
        for count in plan.position_count
    ]
    out = pl.pallas_call(
        functools.partial(table_kernel, plan),
        grid=(1,),
        in_specs=[tail] * plan.n,
        out_specs=[pl.BlockSpec(x.shape, lambda i: (0, 0, 0)) for x in shapes * 2],
        out_shape=shapes * 2,
        scratch_shapes=[pltpu.VMEM((plan.n, plan.row_pad, LANES), jnp.float32)],
        compiler_params=pltpu.CompilerParams(vmem_limit_bytes=VMEM_LIMIT),
        cost_estimate=pl.CostEstimate(flops=10**9, bytes_accessed=10**7, transcendentals=0),
        name="wave_table",
    )(*pieces)
    parts = len(plan.sizes)
    return list(zip(out[:parts], out[parts:]))


def split_kernel(plan, *refs):
    pieces, (high, low) = refs[: plan.n], refs[plan.n :]

    def put(rows, lanes, value):
        top = value.astype(jnp.bfloat16)
        high[rows, lanes] = top
        low[rows, lanes] = (value - top.astype(jnp.float32)).astype(jnp.bfloat16)

    base = plan.n * plan.full * LANES
    for c in range(plan.per_chunk):
        rows = slice(c * plan.stride, c * plan.stride + plan.row_pad)
        for k in range(plan.n):
            for b in range(plan.full):
                at = (k * plan.full + b) * LANES
                put(rows, slice(at, at + LANES), pieces[k][c * plan.full + b])
        for k in range(0, plan.n, 2):
            at = base + k * HALF
            first, second = pieces[k][plan.blocks - 1], pieces[k + 1][plan.blocks - 1]
            lane = lane_iota(first.shape)
            if c:
                first = pltpu.roll(first, LANES - HALF * c, 1)
            else:
                second = pltpu.roll(second, HALF, 1)
            put(rows, slice(at, at + LANES), jnp.where(lane < HALF, first, second))


def split_call(plan, pieces):
    shape = jax.ShapeDtypeStruct((plan.chunk_circles, plan.depth), jnp.bfloat16)
    return pl.pallas_call(
        functools.partial(split_kernel, plan),
        out_shape=[shape, shape],
        compiler_params=pltpu.CompilerParams(vmem_limit_bytes=VMEM_LIMIT),
        cost_estimate=pl.CostEstimate(flops=10**8, bytes_accessed=10**7, transcendentals=0),
        name="split_circles",
    )(*pieces)


def dft_kernel(plan, th_ref, tl_ref, *refs):
    outs = refs[2 * plan.chunks :]
    count = th_ref.shape[1]
    shape = (plan.n * count, plan.depth)
    th, tl = th_ref[...].reshape(shape), tl_ref[...].reshape(shape)
    for chunk in range(plan.chunks):
        fh, fl = refs[2 * chunk][...], refs[2 * chunk + 1][...]
        dims = (((1,), (1,)), ((), ()))
        dot = functools.partial(
            lax.dot_general, dimension_numbers=dims, preferred_element_type=jnp.float32
        )
        total = dot(th, fh) + (dot(th, fl) + dot(tl, fh))
        lanes = slice(chunk * plan.chunk_circles, (chunk + 1) * plan.chunk_circles)
        for k in range(plan.n):
            outs[k][:, lanes] = total[k * count : (k + 1) * count]


def dft_call(plan, table, circles):
    count = table[0].shape[1]
    flops = 6 * plan.n * count * plan.depth * plan.circles
    return pl.pallas_call(
        functools.partial(dft_kernel, plan),
        out_shape=[jax.ShapeDtypeStruct((count, plan.circles), jnp.float32)] * plan.n,
        compiler_params=pltpu.CompilerParams(vmem_limit_bytes=VMEM_LIMIT),
        cost_estimate=pl.CostEstimate(flops=flops, bytes_accessed=10**7, transcendentals=0),
        name="dft",
    )(*table, *[x for pair in circles for x in pair])


def legendre_kernel(plan, part, wide, buffers, wave_ref, scale_ref, *refs):
    pieces = refs[: plan.n]
    tables = refs[plan.n : plan.n + 2]
    edges = refs[plan.n + 2 : plan.n + 4]
    out_ref, right, held, sems = refs[plan.n + 4 :]
    size, start = plan.sizes[part], plan.starts[part]
    count, offset = plan.position_count[part], plan.position_start[part]
    total = plan.owned * MAXM
    me = lax.axis_index("lon")
    inner = wide - LANES

    def place(p):
        t = p // size
        slot = (plan.share * t) // MAXM + start + lax.rem(p, size)
        column = jnp.minimum(slot, plan.owned - 1) * MAXM
        shift = lax.rem(column, LANES)
        return column - shift, shift

    def copies(p, act):
        base, _ = place(p)
        buffer = lax.rem(p, buffers)
        base = pl.multiple_of(base, LANES)
        for f in range(2):
            sem = sems.at[buffer, f]
            act(
                pltpu.make_async_copy(
                    tables[f].at[:, pl.ds(base, inner)],
                    held.at[buffer, f, :, pl.ds(0, inner)],
                    sem,
                )
            )
            last = pl.multiple_of(base + inner, LANES)
            fits = base + wide <= total

            @pl.when(fits)
            def _():
                act(
                    pltpu.make_async_copy(
                        tables[f].at[:, pl.ds(last, LANES)],
                        held.at[buffer, f, :, pl.ds(inner, LANES)],
                        sems.at[buffer, 2 + f],
                    )
                )

            @pl.when(jnp.logical_not(fits))
            def _():
                act(
                    pltpu.make_async_copy(
                        edges[f],
                        held.at[buffer, f, :, pl.ds(inner, LANES)],
                        sems.at[buffer, 2 + f],
                    )
                )

    for p in range(min(buffers - 1, count)):
        copies(jnp.int32(p), lambda c: c.start())

    per_field = plan.n // 2
    scale = scale_ref[...]
    for k in range(plan.n):
        source = lax.bitwise_xor(me, k)
        field = source // per_field
        sample = lax.rem(source, per_field) * plan.cols
        for cs in range(2):
            factor = jnp.where(field == 0, scale, -1.0 if cs == 0 else 1.0)
            imaginary = field if cs else 1 - field
            for c in range(plan.cols):
                value = pieces[k][cs * count : (cs + 1) * count, c * plan.stride : (c + 1) * plan.stride]
                value = value * factor
                rows = pl.ds(imaginary * S + sample + c, count, stride=2 * S)
                for b in range(plan.stride // LANES):
                    right[field, b, rows, :] = value[:, b * LANES : (b + 1) * LANES]
                if plan.stride % LANES:
                    b = plan.stride // LANES
                    right[field, b, rows, 0:HALF] = value[:, b * LANES :]

    blocks = pl.cdiv(plan.stride, LANES)

    @pl.loop(0, count)
    def _(p):
        @pl.when(p + buffers - 1 < count)
        def _():
            copies(p + buffers - 1, lambda c: c.start())

        copies(p, lambda c: c.wait())
        buffer = lax.rem(p, buffers)
        _, shift = place(p)
        sums = None
        rows = pl.ds(pl.multiple_of(p * 2 * S, 2 * S), 2 * S)
        for f in range(2):
            left = [right[f, b, rows, :] for b in range(blocks)]
            left = jnp.concatenate(left, axis=1)[:, : plan.rows].astype(jnp.bfloat16)
            term = jnp.dot(left, held[buffer, f], preferred_element_type=jnp.float32)
            sums = term if sums is None else sums + term
        sums = pltpu.roll(sums, lax.rem(wide - shift, wide), 1)[:, :inner]
        degree = lane_iota((2 * S, inner))
        wave = wave_ref[offset + p]
        keep = (degree >= wave) & (degree < MAXM) & (wave >= 0)
        out_ref[p] = jnp.where(keep, sums, 0.0)


def legendre_call(plan, part, wave, scale, pieces, tables, edges):
    wide = up(MAXM, LANES) + LANES
    buffers = 4
    count = plan.position_count[part]
    vmem = pl.BlockSpec(memory_space=pltpu.VMEM)
    hbm = pl.BlockSpec(memory_space=pl.ANY)
    blocks = pl.cdiv(plan.stride, LANES)
    return pl.pallas_call(
        functools.partial(legendre_kernel, plan, part, wide, buffers),
        in_specs=[pl.BlockSpec(memory_space=pltpu.SMEM), vmem]
        + [vmem] * plan.n
        + [hbm, hbm]
        + [hbm, hbm],
        out_specs=vmem,
        out_shape=jax.ShapeDtypeStruct((count, 2 * S, wide - LANES), jnp.float32),
        scratch_shapes=[
            pltpu.VMEM((2, blocks, count * 2 * S, LANES), jnp.float32),
            pltpu.VMEM((buffers, 2, plan.rows, wide), jnp.bfloat16),
            pltpu.SemaphoreType.DMA((buffers, 4)),
        ],
        compiler_params=pltpu.CompilerParams(vmem_limit_bytes=VMEM_LIMIT),
        cost_estimate=pl.CostEstimate(
            flops=4 * count * 2 * S * plan.rows * wide,
            bytes_accessed=4 * count * plan.rows * wide,
            transcendentals=0,
        ),
        name="legendre",
    )(wave, scale, *pieces, *tables, *edges)


def exchange(plan, pieces):
    order = sorted(range(1, plan.n), key=lambda k: -k)
    got = {0: pieces[0]}
    for k in order:
        got[k] = lax.ppermute(pieces[k], "lon", [(i, i ^ k) for i in range(plan.n)])
    return [got[k] for k in range(plan.n)]


def body(wind_u, wind_v, vorticity, sample_level, slot_wavenumber, legendre_p, legendre_h):
    rows, lons = wind_u.shape[0], wind_u.shape[1]
    lon_count, lat_count = lax.axis_size("lon"), lax.axis_size("lat")
    plan = Plan(rows, lons, slot_wavenumber.shape[0], lon_count, lat_count)
    row_index = lax.axis_index("lat") * rows + jnp.arange(plan.row_pad, dtype=jnp.int32)
    latitude = (row_index.astype(jnp.float32) + 0.5) * (math.pi / NLAT) - 0.5 * math.pi
    cosine = jnp.cos(latitude)[:, None]
    wave = jnp.concatenate([slot_wavenumber, jnp.full((1,), -1, jnp.int32)])
    picks = [min(s, plan.owned) for s in plan.slots]
    wave = wave[jnp.array(picks, jnp.int32)]
    column = jnp.concatenate(
        [wave.astype(jnp.float32), jnp.full((plan.row_pad - len(picks),), -1.0, jnp.float32)]
    )[:, None]
    fields = [jnp.transpose(x, (0, 2, 1)) for x in (wind_u, wind_v, vorticity)]
    sent = flux_call(plan, sample_level[:, None], cosine, column, *fields)
    n = plan.n
    got = [exchange(plan, sent[i * n : (i + 1) * n]) for i in range(plan.chunks)]
    tables = table_call(plan, got[0])
    circles = [split_call(plan, pieces) for pieces in got]
    scale = (jnp.maximum(wave, 0).astype(jnp.float32) / MAXM)[:, None]
    edge_start = plan.owned * MAXM // LANES * LANES
    edges = []
    for table in (legendre_p, legendre_h):
        edge = table[:, edge_start:]
        edges.append(jnp.pad(edge, ((0, 0), (0, LANES - edge.shape[1]))))
    onehot = (sample_level[:, None] == jnp.arange(LEV, dtype=jnp.int32)[None, :]).astype(
        jnp.float32
    )
    powers = []
    for part, size in enumerate(plan.sizes):
        coeffs = exchange(plan, dft_call(plan, tables[part], circles))
        first, count = plan.position_start[part], plan.position_count[part]
        sums = legendre_call(
            plan, part, wave, scale[first : first + count], coeffs, (legendre_p, legendre_h), edges
        )
        mine = lax.psum_scatter(sums, "lat", scatter_dimension=0, tiled=True)
        power = mine[:, :S] ** 2 + mine[:, S:] ** 2
        powers.append(
            jnp.einsum("isx,sl->lix", power, onehot, precision=lax.Precision.HIGHEST) / DAYS
        )
    spectra = jnp.concatenate(powers, axis=1)[:, :, :MAXM].reshape(LEV, plan.cover * MAXM)
    begin = jnp.array([plan.share * t - f * MAXM for t, f in enumerate(plan.first)], jnp.int32)
    return lax.dynamic_slice_in_dim(spectra, begin[lax.axis_index("lat")], plan.share, 1)


def solution(mesh):
    placed = (
        P("lat", "lon", None),
        P("lat", "lon", None),
        P("lat", "lon", None),
        P(),
        P("lon"),
        P("lat", "lon"),
        P("lat", "lon"),
    )
    return jax.shard_map(
        body, mesh=mesh, in_specs=placed, out_specs=P(None, ("lon", "lat")), check_vma=False
    )
```

```python
import functools
import math

import jax
import jax.numpy as jnp
import numpy as np
from jax import lax
from jax.experimental import pallas as pl
from jax.experimental.pallas import tpu as pltpu
from jax.sharding import PartitionSpec as P

NLON = 1440
NLAT = 720
MAXM = 720
LEV = 2
DAYS = 8
S = 16
LANES = 128
HALF = 64
VMEM_LIMIT = 56 * 1024 * 1024
PARTS = (10, 8, 5)


def up(value, step):
    return -(-value // step) * step


class Group:
    def __init__(self, start, rows):
        self.start, self.rows = start, rows
        self.row_pad = up(rows, 8)
        self.stride = up(rows, 16)


class Plan:
    def __init__(self, rows, lons, owned, lon_count, lat_count):
        self.rows, self.lons, self.owned = rows, lons, owned
        self.n, self.lat_count = lon_count, lat_count
        self.cols = 2 * S // lon_count
        self.full, self.rem = divmod(lons, LANES)
        assert 0 < self.rem < HALF
        self.tails = -(-self.cols // 2)
        self.blocks = self.cols * self.full + self.tails
        self.depth = lon_count * (self.full * LANES + HALF)
        self.tile = 64 if rows > 64 else up(rows, 16)
        cut = up(rows // 4, self.tile)
        spans = [(0, cut), (cut, rows)] if cut < rows else [(0, rows)]
        self.groups = [Group(a, b - a) for a, b in spans]
        self.share = owned * MAXM // lat_count
        self.first = [self.share * t // MAXM for t in range(lat_count)]
        last = [-(-self.share * (t + 1) // MAXM) for t in range(lat_count)]
        self.cover = max(b - a for a, b in zip(self.first, last))
        weights = PARTS
        cuts = [round(self.cover * sum(weights[:i]) / sum(weights)) for i in range(len(weights) + 1)]
        self.sizes = [b - a for a, b in zip(cuts, cuts[1:]) if b > a]
        self.starts = [sum(self.sizes[:i]) for i in range(len(self.sizes))]
        self.position_count = [lat_count * s for s in self.sizes]
        self.position_start = [lat_count * s for s in self.starts]
        slots = []
        for start, size in zip(self.starts, self.sizes):
            for t in range(lat_count):
                slots += [self.first[t] + start + i for i in range(size)]
        self.slots = slots
        self.positions = len(slots)
        self.height = self.groups[0].row_pad
        assert self.positions <= 2 * self.height
        self.held_rows = 2 * self.height
        pick = np.zeros((self.held_rows, owned), np.float32)
        absent = np.full((self.held_rows, 1), -1.0, np.float32)
        for p, slot in enumerate(slots):
            if slot < owned:
                pick[p, slot], absent[p] = 1.0, 0.0
        self.pick, self.absent = pick, absent


def lane_iota(shape):
    return lax.broadcasted_iota(jnp.int32, shape, len(shape) - 1)


def cost(us):
    return pl.CostEstimate(flops=0, bytes_accessed=int(us * 3.6e6), transcendentals=0)


def sincos(x):
    r = x - NLON * jnp.floor(x * (1.0 / NLON) + 0.5)
    q = jnp.floor(r * (4.0 / NLON) + 0.5)
    t = (r - q * (NLON // 4)) * (2.0 * math.pi / NLON)
    t2 = t * t
    s = t * (1.0 + t2 * (-1.0 / 6 + t2 * (1.0 / 120 + t2 * (-1.0 / 5040 + t2 * (1.0 / 362880)))))
    c = 1.0 + t2 * (
        -0.5 + t2 * (1.0 / 24 + t2 * (-1.0 / 720 + t2 * (1.0 / 40320 + t2 * (-1.0 / 3628800))))
    )
    size = jnp.abs(q)
    odd, flip = size == 1.0, size == 2.0
    cosine = jnp.where(odd, -q * s, jnp.where(flip, -c, c))
    sine = jnp.where(odd, q * c, jnp.where(flip, -s, s))
    return cosine, sine


def flux_kernel(plan, group, lev_ref, slot_ref, pick_ref, absent_ref, u_ref, v_ref, z_ref, *refs):
    out, scratch = refs
    tile = plan.tile
    row = lax.broadcasted_iota(jnp.int32, (S, 1), 0)
    level = jnp.zeros((S, 1), jnp.int32)
    for s in range(S):
        level = jnp.where(row == s, lev_ref[s], level)

    def eddy(x):
        out = x
        for a in range(LEV):
            mask = (level == a).astype(jnp.float32)[None]
            mean = jnp.sum(x * mask, axis=1, keepdims=True) * (1.0 / DAYS)
            out = out - mean * mask
        return out

    eddy_z = eddy(z_ref[...])
    for f, ref in enumerate((u_ref, v_ref)):
        flux = eddy(ref[...]) * eddy_z
        for b in range(plan.full):
            part = flux[:, :, b * LANES : (b + 1) * LANES]
            scratch[f, b] = part.reshape(tile * S, LANES)
        part = flux[:, :, plan.full * LANES :]
        scratch[f, plan.full, :, 0 : plan.rem] = part.reshape(tile * S, plan.rem)
    first = lax.axis_index("lat") * plan.rows + group.start + pl.program_id(0) * tile
    index = first + lax.broadcasted_iota(jnp.int32, (tile, 1), 0)
    _, cosine = sincos((index.astype(jnp.float32) + 0.5) * (NLON / (2.0 * NLAT)))
    lane = lane_iota((tile, LANES))
    per_field = plan.n // 2
    if group.start == 0:
        wave = slot_ref[...].astype(jnp.float32)
        column = jnp.sum(pick_ref[...] * wave, axis=1, keepdims=True) + absent_ref[...]
    for k in range(plan.n):
        field, sample = k // per_field, k % per_field * plan.cols
        packed = [jnp.zeros((tile, LANES), jnp.float32) for _ in range(plan.tails)]
        for c in range(plan.cols):
            rows = pl.ds(sample + c, tile, stride=S)
            for b in range(plan.full):
                out[k, c * plan.full + b] = scratch[field, b, rows, :] * cosine
            tail = jnp.where(lane < plan.rem, scratch[field, plan.full, rows, :] * cosine, 0.0)
            if c % 2:
                tail = pltpu.roll(tail, HALF, 1)
            packed[c // 2] = packed[c // 2] + tail
        if group.start == 0:
            for i in range(2):
                spare = (lane == (i + 1) * HALF - 1)[: plan.height]
                held = column[i * plan.height : (i + 1) * plan.height]
                packed[0] = jnp.where(spare, held, packed[0][: plan.height])
        for i, value in enumerate(packed):
            out[k, plan.cols * plan.full + i] = value


def flux_call(plan, group, level, slots, u, v, z):
    tile = plan.tile
    skip = group.start // tile
    if skip == 0:
        assert group.row_pad == tile
    field = pl.BlockSpec((tile, S, plan.lons), lambda i: (i + skip, 0, 0))
    fixed = lambda x: pl.BlockSpec(x.shape, lambda i: (0, 0))
    pick, absent = jnp.asarray(plan.pick), jnp.asarray(plan.absent)
    return pl.pallas_call(
        functools.partial(flux_kernel, plan, group),
        grid=(pl.cdiv(group.row_pad, tile),),
        in_specs=[pl.BlockSpec(memory_space=pltpu.SMEM)]
        + [fixed(x) for x in (slots, pick, absent)]
        + [field] * 3,
        out_specs=pl.BlockSpec((plan.n, plan.blocks, tile, LANES), lambda i: (0, 0, i, 0)),
        out_shape=jax.ShapeDtypeStruct(
            (plan.n, plan.blocks, group.row_pad, LANES), jnp.float32
        ),
        scratch_shapes=[pltpu.VMEM((2, plan.full + 1, tile * S, LANES), jnp.float32)],
        compiler_params=pltpu.CompilerParams(vmem_limit_bytes=VMEM_LIMIT),
        cost_estimate=cost(4 * group.rows / 48),
        name="eddy_flux",
    )(level, slots, pick, absent, u, v, z)


def table_kernel(plan, got_ref, *refs):
    parts = len(plan.sizes)
    highs, lows, held = refs[:parts], refs[parts : 2 * parts], refs[-1]
    for k in range(plan.n):
        tail = got_ref[k, 0]
        held[k, 0 : plan.height] = tail
        held[k, plan.height :] = pltpu.roll(tail, HALF, 1)

    @pl.loop(0, plan.n)
    def _(k):
        for j, count in enumerate(plan.position_count):
            start = plan.position_start[j]
            wave = held[k, start : start + count, HALF - 1 : HALF]
            weight = jnp.where(wave >= 0.0, 1.0 / NLON, 0.0)
            wave = jnp.maximum(wave, 0.0)
            lane = lane_iota((count, LANES))
            source = lane.astype(jnp.float32) * plan.lons
            turn_cos, turn_sin = sincos(wave * source)
            base = []
            for b in range(plan.full):
                c, s = sincos(wave * (lane + b * LANES).astype(jnp.float32))
                base.append((c * weight, s * weight))
            tail_lane = lane_iota((count, HALF))
            c, s = sincos(wave * (tail_lane + plan.full * LANES).astype(jnp.float32))
            tail_weight = jnp.where(tail_lane < plan.rem, weight, 0.0)
            c, s = c * tail_weight, s * tail_weight

            def put(where, cosine, sine):
                for row, value in ((0, cosine), (count, sine)):
                    high = value.astype(jnp.bfloat16)
                    highs[j][k, row : row + count, where] = high
                    lows[j][k, row : row + count, where] = (
                        value - high.astype(jnp.float32)
                    ).astype(jnp.bfloat16)

            for src in range(plan.n):
                tc, ts = turn_cos[:, src : src + 1], turn_sin[:, src : src + 1]
                for b in range(plan.full):
                    at = (src * plan.full + b) * LANES
                    bc, bs = base[b]
                    put(slice(at, at + LANES), tc * bc - ts * bs, ts * bc + tc * bs)
            for src in range(0, plan.n, 2):
                at = plan.n * plan.full * LANES + src * HALF
                both = []
                for x in (src, src + 1):
                    tc, ts = turn_cos[:, x : x + 1], turn_sin[:, x : x + 1]
                    both.append((tc * c - ts * s, ts * c + tc * s))
                put(
                    slice(at, at + LANES),
                    jnp.concatenate([both[0][0], both[1][0]], axis=1),
                    jnp.concatenate([both[0][1], both[1][1]], axis=1),
                )


def table_call(plan, got):
    at = plan.cols * plan.full
    tail = pl.BlockSpec((plan.n, 1, plan.height, LANES), lambda i: (0, at, 0, 0))
    shapes = [
        jax.ShapeDtypeStruct((plan.n, 2 * count, plan.depth), jnp.bfloat16)
        for count in plan.position_count
    ]
    out = pl.pallas_call(
        functools.partial(table_kernel, plan),
        grid=(1,),
        in_specs=[tail],
        out_specs=[pl.BlockSpec(x.shape, lambda i: (0, 0, 0)) for x in shapes * 2],
        out_shape=shapes * 2,
        scratch_shapes=[pltpu.VMEM((plan.n, plan.held_rows, LANES), jnp.float32)],
        compiler_params=pltpu.CompilerParams(vmem_limit_bytes=VMEM_LIMIT),
        cost_estimate=cost(12),
        name="wave_table",
    )(got)
    parts = len(plan.sizes)
    return list(zip(out[:parts], out[parts:]))


def split_kernel(plan, group, got_ref, high, low):
    def put(rows, lanes, value):
        top = value.astype(jnp.bfloat16)
        high[rows, lanes] = top
        low[rows, lanes] = (value - top.astype(jnp.float32)).astype(jnp.bfloat16)

    base = plan.n * plan.full * LANES
    for c in range(plan.cols):
        rows = slice(c * group.stride, c * group.stride + group.row_pad)
        for k in range(plan.n):
            for b in range(plan.full):
                at = (k * plan.full + b) * LANES
                put(rows, slice(at, at + LANES), got_ref[k, c * plan.full + b])
        for k in range(0, plan.n, 2):
            at = base + k * HALF
            tail = plan.cols * plan.full + c // 2
            first, second = got_ref[k, tail], got_ref[k + 1, tail]
            lane = lane_iota(first.shape)
            if c % 2:
                first = pltpu.roll(first, HALF, 1)
            else:
                second = pltpu.roll(second, HALF, 1)
            put(rows, slice(at, at + LANES), jnp.where(lane < HALF, first, second))


def split_call(plan, group, got):
    shape = jax.ShapeDtypeStruct((plan.cols * group.stride, plan.depth), jnp.bfloat16)
    return pl.pallas_call(
        functools.partial(split_kernel, plan, group),
        out_shape=[shape, shape],
        compiler_params=pltpu.CompilerParams(vmem_limit_bytes=VMEM_LIMIT),
        cost_estimate=cost(7.0 * group.rows / plan.rows),
        name="split_circles",
    )(got)


def dft_kernel(plan, th_ref, tl_ref, *refs):
    circles, out = refs[:-1], refs[-1]
    count = th_ref.shape[1]
    shape = (plan.n * count, plan.depth)
    th, tl = th_ref[...].reshape(shape), tl_ref[...].reshape(shape)
    dot = functools.partial(
        lax.dot_general,
        dimension_numbers=(((1,), (1,)), ((), ())),
        preferred_element_type=jnp.float32,
    )
    at = 0
    for fh_ref, fl_ref in zip(circles[::2], circles[1::2]):
        fh, fl = fh_ref[...], fl_ref[...]
        total = dot(th, fh) + (dot(th, fl) + dot(tl, fh))
        for k in range(plan.n):
            out[k, :, at : at + fh.shape[0]] = total[k * count : (k + 1) * count]
        at += fh.shape[0]


def dft_call(plan, table, circles):
    count = table[0].shape[1]
    lanes = sum(pair[0].shape[0] for pair in circles)
    return pl.pallas_call(
        functools.partial(dft_kernel, plan),
        out_shape=jax.ShapeDtypeStruct((plan.n, count, lanes), jnp.float32),
        compiler_params=pltpu.CompilerParams(vmem_limit_bytes=VMEM_LIMIT),
        cost_estimate=cost(count * lanes * 27.0 / (184 * 768)),
        name="dft",
    )(*table, *[x for pair in circles for x in pair])


def legendre_kernel(plan, part, wide, buffers, sets, wave_ref, scale_ref, *refs):
    pieces, refs = refs[:sets], refs[sets:]
    tables, edges = refs[:2], refs[2:4]
    send_ref, keep_ref, right, held, sems = refs[4:]
    size, start = plan.sizes[part], plan.starts[part]
    count, offset = plan.position_count[part], plan.position_start[part]
    total = plan.owned * MAXM
    band = lax.axis_index("lat")
    inner = wide - LANES
    step = 2 * LANES
    begins = range(0, wide, step)
    half = count // 2

    def place(p):
        kept = p // half
        q = lax.rem(p, half)
        t = lax.bitwise_xor(q // size * 2 + 1 - kept, band)
        i = lax.rem(q, size)
        slot = (plan.share * t) // MAXM + start + i
        column = jnp.minimum(slot, plan.owned - 1) * MAXM
        shift = lax.rem(column, LANES)
        position = t * size + i
        wave = wave_ref[offset + position]
        lowest = jnp.where(wave < 0, wide, wave + shift) // step
        return position, column - shift, shift, wave, lowest

    def copies(p, act):
        _, base, _, _, lowest = place(p)
        buffer = lax.rem(p, buffers)
        whole = base + wide <= total

        def copy(f, slot, source, at, width):
            into = held.at[buffer, f, :, pl.ds(at, width)]
            act(pltpu.make_async_copy(source, into, sems.at[buffer, f, slot]))

        for i, at in enumerate(begins):

            @pl.when((lowest == i) & whole)
            def _():
                column = pl.multiple_of(base + at, LANES)
                for f in range(2):
                    copy(f, 0, tables[f].at[:, pl.ds(column, wide - at)], at, wide - at)

            @pl.when((lowest == i) & jnp.logical_not(whole))
            def _():
                column = pl.multiple_of(base + at, LANES)
                for f in range(2):
                    if at < inner:
                        copy(f, 0, tables[f].at[:, pl.ds(column, inner - at)], at, inner - at)
                    copy(f, 1, edges[f], inner, LANES)

    for p in range(min(buffers - 1, count)):
        copies(jnp.int32(p), lambda c: c.start())

    per_field = plan.n // 2
    scale = scale_ref[...]
    for k in range(plan.n):
        field, sample = k // per_field, k % per_field * plan.cols
        for cs in range(2):
            factor = (-1.0 if cs == 0 else 1.0) if field else scale
            imaginary = field if cs else 1 - field
            for c in range(plan.cols):
                values = []
                base = 0
                for i, group in enumerate(plan.groups):
                    at = base + c * group.stride
                    block = pieces[i if sets > 1 else 0]
                    values.append(block[k, cs * count : (cs + 1) * count, at : at + group.rows])
                    base += plan.cols * group.stride if sets == 1 else 0
                value = values[0] if len(values) == 1 else jnp.concatenate(values, axis=1)
                value = value * factor
                rows = pl.ds(imaginary * S + sample + c, count, stride=2 * S)
                for b, a in enumerate(range(0, plan.rows, LANES)):
                    width = min(LANES, plan.rows - a)
                    right[field, b, rows, 0:width] = value[:, a : a + width]

    blocks = pl.cdiv(plan.rows, LANES)
    lane = lane_iota((2 * S, LANES))

    def run(first, out_ref):
        @pl.loop(0, half)
        def _(q):
            p = first + q

            @pl.when(p + buffers - 1 < count)
            def _():
                copies(p + buffers - 1, lambda c: c.start())

            copies(p, lambda c: c.wait())
            buffer = lax.rem(p, buffers)
            position, _, shift, wave, lowest = place(p)
            rows = pl.ds(pl.multiple_of(position * 2 * S, 2 * S), 2 * S)

            for i, at in enumerate(begins):

                @pl.when(lowest == i)
                def _():
                    sums = None
                    for f in range(2):
                        row = [right[f, b, rows, :] for b in range(blocks)]
                        left = jnp.concatenate(row, axis=1)[:, : plan.rows].astype(jnp.bfloat16)
                        term = jnp.dot(
                            left, held[buffer, f, :, at:], preferred_element_type=jnp.float32
                        )
                        sums = term if sums is None else sums + term
                    turned = [
                        pltpu.roll(sums[:, v : v + LANES], lax.rem(LANES - shift, LANES), 1)
                        for v in range(0, wide - at, LANES)
                    ]
                    for v in range(inner // LANES):
                        here = slice(v * LANES, (v + 1) * LANES)
                        if (v + 1) * LANES < at:
                            out_ref[q, :, here] = jnp.zeros((2 * S, LANES), jnp.float32)
                            continue
                        w = v - at // LANES
                        below = turned[max(w, 0)]
                        moved = jnp.where(lane < LANES - shift, below, turned[w + 1])
                        degree = lane + v * LANES
                        keep = (degree >= wave) & (degree < MAXM)
                        out_ref[q, :, here] = jnp.where(keep, moved, 0.0)

            @pl.when(wave < 0)
            def _():
                out_ref[q] = jnp.zeros((2 * S, inner), jnp.float32)

    run(0, send_ref)
    run(half, keep_ref)


def legendre_call(plan, part, wave, scale, pieces, tables, edges):
    wide = up(MAXM, LANES) + LANES
    buffers = 8
    count = plan.position_count[part]
    vmem = pl.BlockSpec(memory_space=pltpu.VMEM)
    hbm = pl.BlockSpec(memory_space=pl.ANY)
    blocks = pl.cdiv(plan.rows, LANES)
    shape = jax.ShapeDtypeStruct((count // 2, 2 * S, wide - LANES), jnp.float32)
    return pl.pallas_call(
        functools.partial(legendre_kernel, plan, part, wide, buffers, len(pieces)),
        in_specs=[pl.BlockSpec(memory_space=pltpu.SMEM), vmem]
        + [vmem] * len(pieces)
        + [hbm, hbm]
        + [hbm, hbm],
        out_specs=[vmem, vmem],
        out_shape=[shape, shape],
        scratch_shapes=[
            pltpu.VMEM((2, blocks, count * 2 * S, LANES), jnp.float32),
            pltpu.VMEM((buffers, 2, plan.rows, wide), jnp.bfloat16),
            pltpu.SemaphoreType.DMA((buffers, 2, 2)),
        ],
        compiler_params=pltpu.CompilerParams(vmem_limit_bytes=VMEM_LIMIT),
        cost_estimate=cost(0.6 * count),
        name="legendre",
    )(wave, scale, *pieces, *tables, *edges)


def reduce_scatter(plan, size, send, keep):
    bit = 1
    while True:
        got = lax.ppermute(send, "lat", [(t, t ^ bit) for t in range(plan.lat_count)])
        total = keep + got
        bit *= 2
        if bit == plan.lat_count:
            return total
        total = total.reshape(-1, 2, size, *total.shape[1:])
        send = total[:, 1].reshape(-1, *total.shape[3:])
        keep = total[:, 0].reshape(-1, *total.shape[3:])


def after(x, *others):
    return lax.optimization_barrier((x, *others))[0]


def exchange(x):
    return lax.all_to_all(x, "lon", 0, 0, tiled=True)


def body(wind_u, wind_v, vorticity, sample_level, slot_wavenumber, legendre_p, legendre_h):
    rows, lons = wind_u.shape[0], wind_u.shape[1]
    lon_count, lat_count = lax.axis_size("lon"), lax.axis_size("lat")
    plan = Plan(rows, lons, slot_wavenumber.shape[0], lon_count, lat_count)
    wave = jnp.concatenate([slot_wavenumber, jnp.full((1,), -1, jnp.int32)])
    wave = wave[jnp.array([min(x, plan.owned) for x in plan.slots], jnp.int32)]
    fields = [jnp.transpose(x, (0, 2, 1)) for x in (wind_u, wind_v, vorticity)]
    got = []
    for group in plan.groups:
        sent = flux_call(plan, group, sample_level, slot_wavenumber[None, :], *fields)
        got.append(exchange(after(sent, *got[-1:])))
    tables = table_call(plan, got[0])
    circles = [split_call(plan, group, pieces) for group, pieces in zip(plan.groups, got)]
    scale = (jnp.maximum(wave, 0).astype(jnp.float32) / MAXM)[:, None]
    edge_start = plan.owned * MAXM // LANES * LANES
    edges = []
    for table in (legendre_p, legendre_h):
        edge = table[:, edge_start:]
        edges.append(jnp.pad(edge, ((0, 0), (0, LANES - edge.shape[1]))))
    onehot = (sample_level[:, None] == jnp.arange(LEV, dtype=jnp.int32)[None, :]).astype(
        jnp.float32
    )
    coeffs = []
    for pair in circles:
        sent = dft_call(plan, tables[0], [pair])
        coeffs.append(exchange(after(sent, *(coeffs or got)[-1:])))
    later = [dft_call(plan, table, circles) for table in tables[1:]]
    powers = []
    for part, size in enumerate(plan.sizes):
        first, count = plan.position_start[part], plan.position_count[part]
        following = later[part : part + 1]
        if following:
            following = [exchange(after(following[0], coeffs[-1]))]
        factor = scale[first : first + count]
        send, keep = legendre_call(
            plan, part, wave, factor, coeffs, (legendre_p, legendre_h), edges
        )
        coeffs = following
        mine = reduce_scatter(plan, size, send, keep)
        power = mine[:, :S] ** 2 + mine[:, S:] ** 2
        powers.append(
            jnp.einsum("isx,sl->lix", power, onehot, precision=lax.Precision.HIGHEST) / DAYS
        )
    spectra = jnp.concatenate(powers, axis=1)[:, :, :MAXM].reshape(LEV, plan.cover * MAXM)
    begin = jnp.array([plan.share * t - f * MAXM for t, f in enumerate(plan.first)], jnp.int32)
    return lax.dynamic_slice_in_dim(spectra, begin[lax.axis_index("lat")], plan.share, 1)


def solution(mesh):
    placed = (
        P("lat", "lon", None),
        P("lat", "lon", None),
        P("lat", "lon", None),
        P(),
        P("lon"),
        P("lat", "lon"),
        P("lat", "lon"),
    )
    return jax.shard_map(
        body, mesh=mesh, in_specs=placed, out_specs=P(None, ("lon", "lat")), check_vma=False
    )
```

```python
import functools
import math

import jax
import jax.numpy as jnp
import numpy as np
from jax import lax
from jax.experimental import pallas as pl
from jax.experimental.pallas import tpu as pltpu
from jax.sharding import PartitionSpec as P

NLON = 1440
NLAT = 720
MAXM = 720
LEV = 2
DAYS = 8
S = 16
LANES = 128
HALF = 64
VMEM_LIMIT = 56 * 1024 * 1024
PARTS = (9, 9, 5)


def up(value, step):
    return -(-value // step) * step


class Group:
    def __init__(self, start, rows):
        self.start, self.rows = start, rows
        self.row_pad = up(rows, 8)
        self.stride = up(rows, 16)


class Plan:
    def __init__(self, rows, lons, owned, lon_count, lat_count):
        self.rows, self.lons, self.owned = rows, lons, owned
        self.n, self.lat_count = lon_count, lat_count
        self.cols = 2 * S // lon_count
        self.full, self.rem = divmod(lons, LANES)
        assert 0 < self.rem < HALF
        self.tails = -(-self.cols // 2)
        self.blocks = self.cols * self.full + self.tails
        self.depth = lon_count * (self.full * LANES + HALF)
        self.tile = 64 if rows > 64 else up(rows, 16)
        cut = up(rows // 4, self.tile)
        spans = [(0, cut), (cut, rows)] if cut < rows else [(0, rows)]
        self.groups = [Group(a, b - a) for a, b in spans]
        self.share = owned * MAXM // lat_count
        self.first = [self.share * t // MAXM for t in range(lat_count)]
        last = [-(-self.share * (t + 1) // MAXM) for t in range(lat_count)]
        self.cover = max(b - a for a, b in zip(self.first, last))
        weights = PARTS
        cuts = [round(self.cover * sum(weights[:i]) / sum(weights)) for i in range(len(weights) + 1)]
        self.sizes = [b - a for a, b in zip(cuts, cuts[1:]) if b > a]
        self.starts = [sum(self.sizes[:i]) for i in range(len(self.sizes))]
        self.position_count = [lat_count * s for s in self.sizes]
        self.position_start = [lat_count * s for s in self.starts]
        slots = []
        for start, size in zip(self.starts, self.sizes):
            for t in range(lat_count):
                slots += [self.first[t] + start + i for i in range(size)]
        self.slots = slots
        self.positions = len(slots)
        self.height = self.groups[0].row_pad
        assert self.positions <= 2 * self.height
        self.held_rows = 2 * self.height
        pick = np.zeros((self.held_rows, owned), np.float32)
        absent = np.full((self.held_rows, 1), -1.0, np.float32)
        for p, slot in enumerate(slots):
            if slot < owned:
                pick[p, slot], absent[p] = 1.0, 0.0
        self.pick, self.absent = pick, absent


def lane_iota(shape):
    return lax.broadcasted_iota(jnp.int32, shape, len(shape) - 1)


def cost(us):
    return pl.CostEstimate(flops=0, bytes_accessed=int(us * 3.6e6), transcendentals=0)


def sincos(x):
    r = x - NLON * jnp.floor(x * (1.0 / NLON) + 0.5)
    q = jnp.floor(r * (4.0 / NLON) + 0.5)
    t = (r - q * (NLON // 4)) * (2.0 * math.pi / NLON)
    t2 = t * t
    s = t * (1.0 + t2 * (-1.0 / 6 + t2 * (1.0 / 120 + t2 * (-1.0 / 5040 + t2 * (1.0 / 362880)))))
    c = 1.0 + t2 * (
        -0.5 + t2 * (1.0 / 24 + t2 * (-1.0 / 720 + t2 * (1.0 / 40320 + t2 * (-1.0 / 3628800))))
    )
    size = jnp.abs(q)
    odd, flip = size == 1.0, size == 2.0
    cosine = jnp.where(odd, -q * s, jnp.where(flip, -c, c))
    sine = jnp.where(odd, q * c, jnp.where(flip, -s, s))
    return cosine, sine


def flux_kernel(plan, group, lev_ref, slot_ref, pick_ref, absent_ref, u_ref, v_ref, z_ref, *refs):
    out, scratch = refs
    tile = plan.tile
    row = lax.broadcasted_iota(jnp.int32, (S, 1), 0)
    level = jnp.zeros((S, 1), jnp.int32)
    for s in range(S):
        level = jnp.where(row == s, lev_ref[s], level)

    def eddy(x):
        out = x
        for a in range(LEV):
            mask = (level == a).astype(jnp.float32)[None]
            mean = jnp.sum(x * mask, axis=1, keepdims=True) * (1.0 / DAYS)
            out = out - mean * mask
        return out

    eddy_z = eddy(z_ref[...])
    for f, ref in enumerate((u_ref, v_ref)):
        flux = eddy(ref[...]) * eddy_z
        for b in range(plan.full):
            part = flux[:, :, b * LANES : (b + 1) * LANES]
            scratch[f, b] = part.reshape(tile * S, LANES)
        part = flux[:, :, plan.full * LANES :]
        scratch[f, plan.full, :, 0 : plan.rem] = part.reshape(tile * S, plan.rem)
    first = lax.axis_index("lat") * plan.rows + group.start + pl.program_id(0) * tile
    index = first + lax.broadcasted_iota(jnp.int32, (tile, 1), 0)
    _, cosine = sincos((index.astype(jnp.float32) + 0.5) * (NLON / (2.0 * NLAT)))
    lane = lane_iota((tile, LANES))
    per_field = plan.n // 2
    if group.start == 0:
        wave = slot_ref[...].astype(jnp.float32)
        column = jnp.sum(pick_ref[...] * wave, axis=1, keepdims=True) + absent_ref[...]
    for k in range(plan.n):
        field, sample = k // per_field, k % per_field * plan.cols
        packed = [jnp.zeros((tile, LANES), jnp.float32) for _ in range(plan.tails)]
        for c in range(plan.cols):
            rows = pl.ds(sample + c, tile, stride=S)
            for b in range(plan.full):
                out[k, c * plan.full + b] = scratch[field, b, rows, :] * cosine
            tail = jnp.where(lane < plan.rem, scratch[field, plan.full, rows, :] * cosine, 0.0)
            if c % 2:
                tail = pltpu.roll(tail, HALF, 1)
            packed[c // 2] = packed[c // 2] + tail
        if group.start == 0:
            for i in range(2):
                spare = (lane == (i + 1) * HALF - 1)[: plan.height]
                held = column[i * plan.height : (i + 1) * plan.height]
                packed[0] = jnp.where(spare, held, packed[0][: plan.height])
        for i, value in enumerate(packed):
            out[k, plan.cols * plan.full + i] = value


def flux_call(plan, group, level, slots, u, v, z):
    tile = plan.tile
    skip = group.start // tile
    if skip == 0:
        assert group.row_pad == tile
    field = pl.BlockSpec((tile, S, plan.lons), lambda i: (i + skip, 0, 0))
    fixed = lambda x: pl.BlockSpec(x.shape, lambda i: (0, 0))
    pick, absent = jnp.asarray(plan.pick), jnp.asarray(plan.absent)
    return pl.pallas_call(
        functools.partial(flux_kernel, plan, group),
        grid=(pl.cdiv(group.row_pad, tile),),
        in_specs=[pl.BlockSpec(memory_space=pltpu.SMEM)]
        + [fixed(x) for x in (slots, pick, absent)]
        + [field] * 3,
        out_specs=pl.BlockSpec((plan.n, plan.blocks, tile, LANES), lambda i: (0, 0, i, 0)),
        out_shape=jax.ShapeDtypeStruct(
            (plan.n, plan.blocks, group.row_pad, LANES), jnp.float32
        ),
        scratch_shapes=[pltpu.VMEM((2, plan.full + 1, tile * S, LANES), jnp.float32)],
        compiler_params=pltpu.CompilerParams(vmem_limit_bytes=VMEM_LIMIT),
        cost_estimate=cost(4 * group.rows / 48),
        name="eddy_flux",
    )(level, slots, pick, absent, u, v, z)


def table_kernel(plan, got_ref, *refs):
    parts = len(plan.sizes)
    highs, lows, held = refs[:parts], refs[parts : 2 * parts], refs[-1]
    for k in range(plan.n):
        tail = got_ref[k, 0]
        held[k, 0 : plan.height] = tail
        held[k, plan.height :] = pltpu.roll(tail, HALF, 1)

    @pl.loop(0, plan.n)
    def _(k):
        for j, count in enumerate(plan.position_count):
            start = plan.position_start[j]
            wave = held[k, start : start + count, HALF - 1 : HALF]
            weight = jnp.where(wave >= 0.0, 1.0 / NLON, 0.0)
            wave = jnp.maximum(wave, 0.0)
            lane = lane_iota((count, LANES))
            source = lane.astype(jnp.float32) * plan.lons
            turn_cos, turn_sin = sincos(wave * source)
            base = []
            for b in range(plan.full):
                c, s = sincos(wave * (lane + b * LANES).astype(jnp.float32))
                base.append((c * weight, s * weight))
            tail_lane = lane_iota((count, HALF))
            c, s = sincos(wave * (tail_lane + plan.full * LANES).astype(jnp.float32))
            tail_weight = jnp.where(tail_lane < plan.rem, weight, 0.0)
            c, s = c * tail_weight, s * tail_weight

            def put(where, cosine, sine):
                for row, value in ((0, cosine), (count, sine)):
                    high = value.astype(jnp.bfloat16)
                    highs[j][k, row : row + count, where] = high
                    lows[j][k, row : row + count, where] = (
                        value - high.astype(jnp.float32)
                    ).astype(jnp.bfloat16)

            for src in range(plan.n):
                tc, ts = turn_cos[:, src : src + 1], turn_sin[:, src : src + 1]
                for b in range(plan.full):
                    at = (src * plan.full + b) * LANES
                    bc, bs = base[b]
                    put(slice(at, at + LANES), tc * bc - ts * bs, ts * bc + tc * bs)
            for src in range(0, plan.n, 2):
                at = plan.n * plan.full * LANES + src * HALF
                both = []
                for x in (src, src + 1):
                    tc, ts = turn_cos[:, x : x + 1], turn_sin[:, x : x + 1]
                    both.append((tc * c - ts * s, ts * c + tc * s))
                put(
                    slice(at, at + LANES),
                    jnp.concatenate([both[0][0], both[1][0]], axis=1),
                    jnp.concatenate([both[0][1], both[1][1]], axis=1),
                )


def table_call(plan, got):
    at = plan.cols * plan.full
    tail = pl.BlockSpec((plan.n, 1, plan.height, LANES), lambda i: (0, at, 0, 0))
    shapes = [
        jax.ShapeDtypeStruct((plan.n, 2 * count, plan.depth), jnp.bfloat16)
        for count in plan.position_count
    ]
    out = pl.pallas_call(
        functools.partial(table_kernel, plan),
        grid=(1,),
        in_specs=[tail],
        out_specs=[pl.BlockSpec(x.shape, lambda i: (0, 0, 0)) for x in shapes * 2],
        out_shape=shapes * 2,
        scratch_shapes=[pltpu.VMEM((plan.n, plan.held_rows, LANES), jnp.float32)],
        compiler_params=pltpu.CompilerParams(vmem_limit_bytes=VMEM_LIMIT),
        cost_estimate=cost(12),
        name="wave_table",
    )(got)
    parts = len(plan.sizes)
    return list(zip(out[:parts], out[parts:]))


def split_kernel(plan, group, got_ref, high, low):
    def put(rows, lanes, value):
        top = value.astype(jnp.bfloat16)
        high[rows, lanes] = top
        low[rows, lanes] = (value - top.astype(jnp.float32)).astype(jnp.bfloat16)

    base = plan.n * plan.full * LANES
    for c in range(plan.cols):
        rows = slice(c * group.stride, c * group.stride + group.row_pad)
        for k in range(plan.n):
            for b in range(plan.full):
                at = (k * plan.full + b) * LANES
                put(rows, slice(at, at + LANES), got_ref[k, c * plan.full + b])
        for k in range(0, plan.n, 2):
            at = base + k * HALF
            tail = plan.cols * plan.full + c // 2
            first, second = got_ref[k, tail], got_ref[k + 1, tail]
            lane = lane_iota(first.shape)
            if c % 2:
                first = pltpu.roll(first, HALF, 1)
            else:
                second = pltpu.roll(second, HALF, 1)
            put(rows, slice(at, at + LANES), jnp.where(lane < HALF, first, second))


def split_call(plan, group, got):
    shape = jax.ShapeDtypeStruct((plan.cols * group.stride, plan.depth), jnp.bfloat16)
    return pl.pallas_call(
        functools.partial(split_kernel, plan, group),
        out_shape=[shape, shape],
        compiler_params=pltpu.CompilerParams(vmem_limit_bytes=VMEM_LIMIT),
        cost_estimate=cost(7.0 * group.rows / plan.rows),
        name="split_circles",
    )(got)


def dft_kernel(plan, th_ref, tl_ref, *refs):
    circles, out = refs[:-1], refs[-1]
    count = th_ref.shape[1]
    shape = (plan.n * count, plan.depth)
    th, tl = th_ref[...].reshape(shape), tl_ref[...].reshape(shape)
    dot = functools.partial(
        lax.dot_general,
        dimension_numbers=(((1,), (1,)), ((), ())),
        preferred_element_type=jnp.float32,
    )
    at = 0
    for fh_ref, fl_ref in zip(circles[::2], circles[1::2]):
        fh, fl = fh_ref[...], fl_ref[...]
        total = dot(th, fh) + (dot(th, fl) + dot(tl, fh))
        for k in range(plan.n):
            out[k, :, at : at + fh.shape[0]] = total[k * count : (k + 1) * count]
        at += fh.shape[0]


def dft_call(plan, table, circles):
    count = table[0].shape[1]
    lanes = sum(pair[0].shape[0] for pair in circles)
    return pl.pallas_call(
        functools.partial(dft_kernel, plan),
        out_shape=jax.ShapeDtypeStruct((plan.n, count, lanes), jnp.float32),
        compiler_params=pltpu.CompilerParams(vmem_limit_bytes=VMEM_LIMIT),
        cost_estimate=cost(count * lanes * 27.0 / (184 * 768)),
        name="dft",
    )(*table, *[x for pair in circles for x in pair])


def legendre_kernel(plan, part, wide, buffers, sets, wave_ref, scale_ref, *refs):
    pieces, refs = refs[:sets], refs[sets:]
    tables, edges = refs[:2], refs[2:4]
    send_ref, keep_ref, right, held, sems = refs[4:]
    size, start = plan.sizes[part], plan.starts[part]
    count, offset = plan.position_count[part], plan.position_start[part]
    total = plan.owned * MAXM
    band = lax.axis_index("lat")
    inner = wide - LANES
    step = 2 * LANES
    begins = range(0, wide, step)
    half = count // 2

    def place(p):
        kept = p // half
        q = lax.rem(p, half)
        t = lax.bitwise_xor(q // size * 2 + 1 - kept, band)
        i = lax.rem(q, size)
        slot = (plan.share * t) // MAXM + start + i
        column = jnp.minimum(slot, plan.owned - 1) * MAXM
        shift = lax.rem(column, LANES)
        position = t * size + i
        wave = wave_ref[offset + position]
        lowest = jnp.where(wave < 0, wide, wave + shift) // step
        return position, column - shift, shift, wave, lowest

    def copies(p, act):
        _, base, _, _, lowest = place(p)
        buffer = lax.rem(p, buffers)
        whole = base + wide <= total

        def copy(f, slot, source, at, width):
            into = held.at[buffer, f, :, pl.ds(at, width)]
            act(pltpu.make_async_copy(source, into, sems.at[buffer, f, slot]))

        for i, at in enumerate(begins):

            @pl.when((lowest == i) & whole)
            def _():
                column = pl.multiple_of(base + at, LANES)
                for f in range(2):
                    copy(f, 0, tables[f].at[:, pl.ds(column, wide - at)], at, wide - at)

            @pl.when((lowest == i) & jnp.logical_not(whole))
            def _():
                column = pl.multiple_of(base + at, LANES)
                for f in range(2):
                    if at < inner:
                        copy(f, 0, tables[f].at[:, pl.ds(column, inner - at)], at, inner - at)
                    copy(f, 1, edges[f], inner, LANES)

    for p in range(min(buffers - 1, count)):
        copies(jnp.int32(p), lambda c: c.start())

    per_field = plan.n // 2
    scale = scale_ref[...]
    for k in range(plan.n):
        field, sample = k // per_field, k % per_field * plan.cols
        for cs in range(2):
            factor = (-1.0 if cs == 0 else 1.0) if field else scale
            imaginary = field if cs else 1 - field
            for c in range(plan.cols):
                values = []
                base = 0
                for i, group in enumerate(plan.groups):
                    at = base + c * group.stride
                    block = pieces[i if sets > 1 else 0]
                    values.append(block[k, cs * count : (cs + 1) * count, at : at + group.rows])
                    base += plan.cols * group.stride if sets == 1 else 0
                value = values[0] if len(values) == 1 else jnp.concatenate(values, axis=1)
                value = value * factor
                rows = pl.ds(imaginary * S + sample + c, count, stride=2 * S)
                for b, a in enumerate(range(0, plan.rows, LANES)):
                    width = min(LANES, plan.rows - a)
                    right[field, b, rows, 0:width] = value[:, a : a + width]

    blocks = pl.cdiv(plan.rows, LANES)
    lane = lane_iota((2 * S, LANES))

    def run(first, out_ref):
        @pl.loop(0, half)
        def _(q):
            p = first + q

            @pl.when(p + buffers - 1 < count)
            def _():
                copies(p + buffers - 1, lambda c: c.start())

            copies(p, lambda c: c.wait())
            buffer = lax.rem(p, buffers)
            position, _, shift, wave, lowest = place(p)
            rows = pl.ds(pl.multiple_of(position * 2 * S, 2 * S), 2 * S)

            for i, at in enumerate(begins):

                @pl.when(lowest == i)
                def _():
                    sums = None
                    for f in range(2):
                        row = [right[f, b, rows, :] for b in range(blocks)]
                        left = jnp.concatenate(row, axis=1)[:, : plan.rows].astype(jnp.bfloat16)
                        term = jnp.dot(
                            left, held[buffer, f, :, at:], preferred_element_type=jnp.float32
                        )
                        sums = term if sums is None else sums + term
                    turned = [
                        pltpu.roll(sums[:, v : v + LANES], lax.rem(LANES - shift, LANES), 1)
                        for v in range(0, wide - at, LANES)
                    ]
                    for v in range(inner // LANES):
                        here = slice(v * LANES, (v + 1) * LANES)
                        if (v + 1) * LANES < at:
                            out_ref[q, :, here] = jnp.zeros((2 * S, LANES), jnp.float32)
                            continue
                        w = v - at // LANES
                        below = turned[max(w, 0)]
                        moved = jnp.where(lane < LANES - shift, below, turned[w + 1])
                        degree = lane + v * LANES
                        keep = (degree >= wave) & (degree < MAXM)
                        out_ref[q, :, here] = jnp.where(keep, moved, 0.0)

            @pl.when(wave < 0)
            def _():
                out_ref[q] = jnp.zeros((2 * S, inner), jnp.float32)

    run(0, send_ref)
    run(half, keep_ref)


def legendre_call(plan, part, wave, scale, pieces, tables, edges):
    wide = up(MAXM, LANES) + LANES
    buffers = 8
    count = plan.position_count[part]
    vmem = pl.BlockSpec(memory_space=pltpu.VMEM)
    hbm = pl.BlockSpec(memory_space=pl.ANY)
    blocks = pl.cdiv(plan.rows, LANES)
    shape = jax.ShapeDtypeStruct((count // 2, 2 * S, wide - LANES), jnp.float32)
    return pl.pallas_call(
        functools.partial(legendre_kernel, plan, part, wide, buffers, len(pieces)),
        in_specs=[pl.BlockSpec(memory_space=pltpu.SMEM), vmem]
        + [vmem] * len(pieces)
        + [hbm, hbm]
        + [hbm, hbm],
        out_specs=[vmem, vmem],
        out_shape=[shape, shape],
        scratch_shapes=[
            pltpu.VMEM((2, blocks, count * 2 * S, LANES), jnp.float32),
            pltpu.VMEM((buffers, 2, plan.rows, wide), jnp.bfloat16),
            pltpu.SemaphoreType.DMA((buffers, 2, 2)),
        ],
        compiler_params=pltpu.CompilerParams(vmem_limit_bytes=VMEM_LIMIT),
        cost_estimate=cost(0.6 * count),
        name="legendre",
    )(wave, scale, *pieces, *tables, *edges)


def reduce_scatter(plan, size, send, keep):
    bit = 1
    while True:
        got = lax.ppermute(send, "lat", [(t, t ^ bit) for t in range(plan.lat_count)])
        total = keep + got
        bit *= 2
        if bit == plan.lat_count:
            return total
        total = total.reshape(-1, 2, size, *total.shape[1:])
        send = total[:, 1].reshape(-1, *total.shape[3:])
        keep = total[:, 0].reshape(-1, *total.shape[3:])


def after(x, *others):
    return lax.optimization_barrier((x, *others))[0]


def exchange(x):
    return lax.all_to_all(x, "lon", 0, 0, tiled=True)


def body(wind_u, wind_v, vorticity, sample_level, slot_wavenumber, legendre_p, legendre_h):
    rows, lons = wind_u.shape[0], wind_u.shape[1]
    lon_count, lat_count = lax.axis_size("lon"), lax.axis_size("lat")
    plan = Plan(rows, lons, slot_wavenumber.shape[0], lon_count, lat_count)
    wave = jnp.concatenate([slot_wavenumber, jnp.full((1,), -1, jnp.int32)])
    wave = wave[jnp.array([min(x, plan.owned) for x in plan.slots], jnp.int32)]
    fields = [jnp.transpose(x, (0, 2, 1)) for x in (wind_u, wind_v, vorticity)]
    got = []
    for group in plan.groups:
        sent = flux_call(plan, group, sample_level, slot_wavenumber[None, :], *fields)
        got.append(exchange(after(sent, *got[-1:])))
    tables = table_call(plan, got[0])
    circles = [split_call(plan, group, pieces) for group, pieces in zip(plan.groups, got)]
    scale = (jnp.maximum(wave, 0).astype(jnp.float32) / MAXM)[:, None]
    edge_start = plan.owned * MAXM // LANES * LANES
    edges = []
    for table in (legendre_p, legendre_h):
        edge = table[:, edge_start:]
        edges.append(jnp.pad(edge, ((0, 0), (0, LANES - edge.shape[1]))))
    onehot = (sample_level[:, None] == jnp.arange(LEV, dtype=jnp.int32)[None, :]).astype(
        jnp.float32
    )
    coeffs = []
    for pair in circles:
        sent = dft_call(plan, tables[0], [pair])
        coeffs.append(exchange(after(sent, *(coeffs or got)[-1:])))
    later = [dft_call(plan, table, circles) for table in tables[1:]]
    powers = []
    for part, size in enumerate(plan.sizes):
        first, count = plan.position_start[part], plan.position_count[part]
        following = later[part : part + 1]
        if following:
            following = [exchange(after(following[0], coeffs[-1]))]
        factor = scale[first : first + count]
        send, keep = legendre_call(
            plan, part, wave, factor, coeffs, (legendre_p, legendre_h), edges
        )
        coeffs = following
        mine = reduce_scatter(plan, size, send, keep)
        power = mine[:, :S] ** 2 + mine[:, S:] ** 2
        powers.append(
            jnp.einsum("isx,sl->lix", power, onehot, precision=lax.Precision.HIGHEST) / DAYS
        )
    spectra = jnp.concatenate(powers, axis=1)[:, :, :MAXM].reshape(LEV, plan.cover * MAXM)
    begin = jnp.array([plan.share * t - f * MAXM for t, f in enumerate(plan.first)], jnp.int32)
    return lax.dynamic_slice_in_dim(spectra, begin[lax.axis_index("lat")], plan.share, 1)


def solution(mesh):
    placed = (
        P("lat", "lon", None),
        P("lat", "lon", None),
        P("lat", "lon", None),
        P(),
        P("lon"),
        P("lat", "lon"),
        P("lat", "lon"),
    )
    return jax.shard_map(
        body, mesh=mesh, in_specs=placed, out_specs=P(None, ("lon", "lat")), check_vma=False
    )
```
